32 devices in a mesh: dp: 8 (over y, x, core), tensor: 4 (over z).
Axes of the slice: x: 2, y: 2, z: 4, core: 2. Of those that a mesh axis runs over, the one named last changes fastest.
Arguments:
- query: bfloat16 [8192, 5120], P('dp', 'tensor'), may hold values from -6 to 6
- keys: bfloat16 [8192, 1024], P('dp', 'tensor'), may hold values from -6 to 6
- values: bfloat16 [8192, 1024], P('dp', 'tensor'), may hold values from -6 to 6
- out_weight: bfloat16 [5120, 2560], P('tensor', 'dp'), may hold values from -0.078125 to 0.078125
- loss_grad: bfloat16 [8192, 2560], P('dp', 'tensor'), may hold values from -6 to 6
- lengths: int32 [8, 16], P('dp'), may hold values from 1 to 512, 1024 in all within a row
- languages: int32 [8, 16], P('dp'), may hold values from 0 to 28
- labels: int32 [8192], P('dp'), may hold values from -100 to 152063, as said below
Outputs:
- attention_result: bfloat16 [8192, 5120], P('dp', 'tensor')
- query_gradient: bfloat16 [8192, 5120], P('dp', 'tensor')
- key_gradient: bfloat16 [8192, 1024], P('dp', 'tensor')
- value_gradient: bfloat16 [8192, 1024], P('dp', 'tensor')
- projection_gradient: bfloat16 [5120, 2560], P('tensor')
The draws below stay inside these ranges and needn't reach their ends.
Inputs may be any that keep to these rules, and one draw needn't show every extreme that they name: `labels`: each label is -100, meaning no loss on that token, or a token id below 152064.
All inputs are finite; a program needn't handle non-finite values.
Results may differ from the reference program's by a relative error of at most 0.02.
Values may be sent and summed in bfloat16 or wider, within the bound.
A program may use at most 192 MiB of HBM per device.

```python
import math
import jax
import jax.numpy as jnp
import numpy as np
from jax import lax

QUERY_HEADS = 40
KEY_VALUE_HEADS = 8
HEAD_SIZE = 128
VOCAB = 152064
DWIN = 2560
LANGS = 29
DOCS = 16
PACK_TOKENS = 1024
TOTAL_TOKENS = 8192
N_DP = 8


def base_sample(key, shape):
    return jnp.clip(jax.random.normal(key, shape), -5.0, 5.0)


def draw_query(key, part):
    base_value = base_sample(jax.random.fold_in(key, 1), (TOTAL_TOKENS, QUERY_HEADS * HEAD_SIZE))
    return base_value.astype(jnp.bfloat16)


def draw_keys(key, part):
    base_value = base_sample(jax.random.fold_in(key, 2), (TOTAL_TOKENS, KEY_VALUE_HEADS * HEAD_SIZE))
    return base_value.astype(jnp.bfloat16)


def draw_labels(key, part):
    rolls = jax.random.randint(jax.random.fold_in(key, 1), (TOTAL_TOKENS,), 0, 10)
    token_ids = jax.random.randint(jax.random.fold_in(key, 2), (TOTAL_TOKENS,), 0, VOCAB)
    places = jnp.arange(TOTAL_TOKENS, dtype=jnp.int32)
    last_row = places == TOTAL_TOKENS - 1
    token_ids = jnp.where(last_row, VOCAB - 1, token_ids)
    return jnp.where((rolls < 3) & jnp.logical_not(last_row), -100, token_ids).astype(jnp.int32)


def set_ends(array, rng, low, largest):
    dims = array.shape
    index_at = [jax.random.randint(jax.random.fold_in(rng, axis), (), 0, dims[axis]) for axis in range(len(dims))]
    array = array.at[tuple(index_at)].set(low)
    longest = dims.index(max(dims))
    index_at[longest] = (index_at[longest] + 1) % dims[longest]
    return array.at[tuple(index_at)].set(largest)


def steps_of(stream_key, dims, split, low, high):
    loudness = 1.0
    for dim, blocks in split:
        steps = jax.random.uniform(jax.random.fold_in(jax.random.fold_in(stream_key, 6), dim), (blocks,), jnp.float32, low / len(split), high / len(split))
        loudness = loudness * jnp.repeat(jnp.exp(steps), dims[dim] // blocks).reshape((-1,) + (1,) * (len(dims) - 1 - dim))
    return loudness


def cumulative_ranks(amount, skew):
    portions = [(1 << 20) // math.isqrt(grade ** skew) + 1 for grade in range(1, amount + 1)]
    deviation = 1 + sum(portions) // (1 << 30)
    return np.cumsum(np.array([max(1, weight // deviation) for weight in portions]))


def skewed_ids(stream_key, dims, amount, lean):
    table = cumulative_ranks(amount, lean)
    pick = jax.random.randint(jax.random.fold_in(stream_key, 1), dims, 0, int(table[amount - 1]))
    rank = jnp.searchsorted(jnp.asarray(table, jnp.int32), pick, side="right")
    return jax.random.permutation(jax.random.fold_in(stream_key, 2), amount)[rank].astype(jnp.int32)


def split_up(number_of, total, most, lean):
    loads = [(1 << 20) // math.isqrt(standing ** lean) + 1 for standing in range(2, number_of + 1)]
    rest, given = total - most - (number_of - 1), [1] * (number_of - 1)
    while rest > 0:
        movable = [i for i in range(number_of - 1) if given[i] < most]
        whole, left = sum([loads[i] for i in movable]), rest
        for i in movable:
            more = min(most - given[i], max(1, left * loads[i] // whole), rest)
            given[i] = given[i] + more
            rest = rest - more
    return np.array([most] + given)


def ragged_sizes(rng, count, total, most, slope):
    if count == 2:
        one = jax.random.randint(rng, (), max(1, total - most), min(most, total - 1) + 1)
        return jnp.stack([one, total - one])
    sizes = jnp.asarray(split_up(count, total, most, slope), jnp.int32)
    couples = (count - 1) // 2
    donor, receiver = sizes[1:1 + 2 * couples:2], sizes[2:2 + 2 * couples:2]
    margin = jnp.minimum(donor - 1, most - receiver)
    moved = jax.random.randint(jax.random.fold_in(rng, 1), (couples,), 0, 1 << 20) % (margin + 1)
    sizes = sizes.at[1:1 + 2 * couples:2].set(donor - moved).at[2:2 + 2 * couples:2].set(receiver + moved)
    return sizes[jax.random.permutation(jax.random.fold_in(rng, 2), count)]


def scatter_about(rng, shape, scale, bound, shards=(), kind=jnp.bfloat16):
    values = jax.random.normal(rng, shape, jnp.float32) * scale
    if len(shards) > 0:
        values = steps_of(rng, shape, shards, -0.22, 0.18) * values
    return jnp.clip(values, min=-bound, max=bound).astype(kind)


def setup_inputs(seed: int = 0) -> dict:
    key_of = jax.random.split(jax.random.key(seed), 9)
    query = draw_query(jax.random.fold_in(key_of[8], 71), 0)
    keys = draw_keys(jax.random.fold_in(key_of[8], 71), 0)
    values = scatter_about(key_of[2], (TOTAL_TOKENS, KEY_VALUE_HEADS * HEAD_SIZE), 1.0, 6.0, ((0, 8), (1, 4)))
    out_weight = scatter_about(key_of[3], (QUERY_HEADS * HEAD_SIZE, DWIN), (QUERY_HEADS * HEAD_SIZE) ** -0.5, 0.078125, ((0, 4), (1, 8)))
    loss_grad = scatter_about(key_of[4], (TOTAL_TOKENS, DWIN), 1.0, 6.0, ((0, 8), (1, 4)))
    lengths = jax.vmap(lambda own: ragged_sizes(own, DOCS, PACK_TOKENS, PACK_TOKENS // 2, 2))(jax.random.split(key_of[5], N_DP)).reshape((N_DP, DOCS)).astype(jnp.int32)
    languages = set_ends(skewed_ids(key_of[6], (N_DP, DOCS), LANGS, 2), jax.random.fold_in(key_of[6], 3), 0, LANGS - 1).astype(jnp.int32)
    labels = draw_labels(jax.random.fold_in(key_of[8], 71), 0)
    return {"query": query, "keys": keys, "values": values, "out_weight": out_weight, "loss_grad": loss_grad, "lengths": lengths, "languages": languages, "labels": labels}


def token_docs(length_row, row_count):
    doc_ends = jnp.cumsum(length_row).astype(jnp.int32)
    places = jnp.arange(row_count, dtype=jnp.int32)
    return lax.optimization_barrier(jnp.sum((places[:, None] >= doc_ends[None, :]).astype(jnp.int32), axis=1))

def masked_scores(query_rows, key_rows, allowed, factor):
    scores = jnp.einsum('rgd,kd->grk', query_rows.astype(jnp.float32), key_rows.astype(jnp.float32)) * factor
    return jnp.where(allowed[None], scores, -1e+30)

def forward_group(query_rows, key_rows, value_rows, allowed, factor):
    scores = masked_scores(query_rows, key_rows, allowed, factor)
    row_top = lax.optimization_barrier(jnp.max(scores, axis=2, keepdims=True))
    log_total = row_top + jnp.log(lax.optimization_barrier(jnp.sum(jnp.exp(scores - row_top), axis=2, keepdims=True)))
    weights = jnp.exp(scores - log_total).astype(jnp.bfloat16)
    result = jnp.einsum('grk,kd->rgd', weights.astype(jnp.float32), value_rows.astype(jnp.float32))
    return (result.astype(jnp.bfloat16), log_total[:, :, 0])

def backward_group(query_rows, key_rows, value_rows, allowed, out_rows, log_rows, grad_rows, factor):
    scores = masked_scores(query_rows, key_rows, allowed, factor)
    weights = jnp.exp(scores - log_rows[:, :, None])
    grad_wide = grad_rows.astype(jnp.float32)
    value_gradient = jnp.einsum('grk,rgd->kd', weights.astype(jnp.bfloat16).astype(jnp.float32), grad_wide)
    weight_grad = jnp.einsum('rgd,kd->grk', grad_wide, value_rows.astype(jnp.float32))
    diagonal_term = jnp.einsum('rgd,rgd->gr', grad_wide, out_rows.astype(jnp.float32))
    score_grad = (weights * (weight_grad - diagonal_term[:, :, None]) * factor).astype(jnp.bfloat16)
    score_wide = score_grad.astype(jnp.float32)
    query_gradient = jnp.einsum('grk,kd->rgd', score_wide, key_rows.astype(jnp.float32))
    key_gradient = jnp.einsum('grk,rgd->kd', score_wide, query_rows.astype(jnp.float32))
    return (query_gradient, key_gradient, value_gradient)

def reference(query, keys, values, out_weight, loss_grad, lengths, languages, labels):
    factor = 1.0 / math.sqrt(HEAD_SIZE)
    group_size = QUERY_HEADS // KEY_VALUE_HEADS
    places = jnp.arange(PACK_TOKENS, dtype=jnp.int32)

    def layout(length_row):
        doc_ids = token_docs(length_row, PACK_TOKENS)
        return (doc_ids[:, None] == doc_ids[None, :]) & (places[:, None] >= places[None, :])

    def pack_forward(item):
        packed_query, key_pack, value_pack, length_row = item
        allowed = layout(length_row)
        query_by_head = packed_query.reshape(PACK_TOKENS, KEY_VALUE_HEADS, group_size, HEAD_SIZE)
        outs = []
        logs = []
        for head_cluster in range(KEY_VALUE_HEADS):
            result, log_rows = forward_group(query_by_head[:, head_cluster], key_pack[:, head_cluster * HEAD_SIZE:(head_cluster + 1) * HEAD_SIZE], value_pack[:, head_cluster * HEAD_SIZE:(head_cluster + 1) * HEAD_SIZE], allowed, factor)
            outs.append(result.reshape(PACK_TOKENS, group_size * HEAD_SIZE))
            logs.append(log_rows)
        return (jnp.concatenate(outs, axis=1), jnp.stack(logs, axis=0))
    query_packs = query.reshape(N_DP, PACK_TOKENS, QUERY_HEADS * HEAD_SIZE)
    packed_keys = keys.reshape(N_DP, PACK_TOKENS, KEY_VALUE_HEADS * HEAD_SIZE)
    packed_values = values.reshape(N_DP, PACK_TOKENS, KEY_VALUE_HEADS * HEAD_SIZE)
    attn_packs, log_packs = lax.map(pack_forward, (query_packs, packed_keys, packed_values, lengths))
    attention_result = attn_packs.reshape(TOTAL_TOKENS, QUERY_HEADS * HEAD_SIZE)
    doc_all = jax.vmap(lambda row: token_docs(row, PACK_TOKENS))(lengths)
    token_lang = jnp.take_along_axis(languages, doc_all, axis=1).reshape(TOTAL_TOKENS)
    counted = labels != -100
    hits = ((token_lang[:, None] == jnp.arange(LANGS, dtype=jnp.int32)[None, :]) & counted[:, None]).astype(jnp.int32)
    counts = lax.optimization_barrier(jnp.sum(hits, axis=0)).astype(jnp.float32)
    lang_weight = jnp.sqrt(jnp.sum(counts) / (LANGS * jnp.maximum(counts, 1.0)))
    token_weight = jnp.where(counted, lang_weight[token_lang], 0.0)
    weighted = (token_weight[:, None] * loss_grad.astype(jnp.float32)).astype(jnp.bfloat16)
    out_grad = jnp.dot(weighted, out_weight.T, preferred_element_type=jnp.float32).astype(jnp.bfloat16)
    projection_gradient = jnp.dot(attention_result.T, weighted, preferred_element_type=jnp.float32).astype(jnp.bfloat16)

    def pack_backward(item):
        packed_query, key_pack, value_pack, length_row, attention_per_pack, log_pack, gradient_per_pack = item
        allowed = layout(length_row)
        query_by_head = packed_query.reshape(PACK_TOKENS, KEY_VALUE_HEADS, group_size, HEAD_SIZE)
        attention_by_head = attention_per_pack.reshape(PACK_TOKENS, KEY_VALUE_HEADS, group_size, HEAD_SIZE)
        gradient_by_head = gradient_per_pack.reshape(PACK_TOKENS, KEY_VALUE_HEADS, group_size, HEAD_SIZE)
        query_parts = []
        key_parts = []
        value_parts = []
        for head_cluster in range(KEY_VALUE_HEADS):
            query_part, key_part, value_part = backward_group(query_by_head[:, head_cluster], key_pack[:, head_cluster * HEAD_SIZE:(head_cluster + 1) * HEAD_SIZE], value_pack[:, head_cluster * HEAD_SIZE:(head_cluster + 1) * HEAD_SIZE], allowed, attention_by_head[:, head_cluster], log_pack[head_cluster], gradient_by_head[:, head_cluster], factor)
            query_parts.append(query_part.astype(jnp.bfloat16).reshape(PACK_TOKENS, group_size * HEAD_SIZE))
            key_parts.append(key_part.astype(jnp.bfloat16))
            value_parts.append(value_part.astype(jnp.bfloat16))
        return (jnp.concatenate(query_parts, axis=1), jnp.concatenate(key_parts, axis=1), jnp.concatenate(value_parts, axis=1))
    query_gradient, key_gradient, value_gradient = lax.map(pack_backward, (query_packs, packed_keys, packed_values, lengths, attn_packs, log_packs, out_grad.reshape(N_DP, PACK_TOKENS, QUERY_HEADS * HEAD_SIZE)))
    return (attention_result, query_gradient.reshape(TOTAL_TOKENS, QUERY_HEADS * HEAD_SIZE), key_gradient.reshape(TOTAL_TOKENS, KEY_VALUE_HEADS * HEAD_SIZE), value_gradient.reshape(TOTAL_TOKENS, KEY_VALUE_HEADS * HEAD_SIZE), projection_gradient)
```

```python
import math

import jax
import jax.numpy as jnp
from jax import lax
from jax.experimental import pallas as pl
from jax.experimental.pallas import tpu as pltpu
from jax.sharding import PartitionSpec as P

QUERY_HEADS = 40
KEY_VALUE_HEADS = 8
HEAD_SIZE = 128
LANGS = 29
DOCS = 16
GROUP = QUERY_HEADS // KEY_VALUE_HEADS
BLOCK = 256
REACH = 512
FACTOR = 1.0 / math.sqrt(HEAD_SIZE)
LOG2E = math.log2(math.e)
NT = (((1,), (1,)), ((), ()))
NN = (((1,), (0,)), ((), ()))
TN = (((0,), (0,)), ((), ()))


def dot(a, b, dims):
    return lax.dot_general(a, b, dims, preferred_element_type=jnp.float32)


def windows(rows):
    return [(at, max(0, at - REACH), at + BLOCK) for at in range(0, rows, BLOCK)]


def fill_bias(starts_ref, bias_ref, rows):
    for index, (at, low, high) in enumerate(windows(rows)):
        shape = (high - low, BLOCK)
        key_place = low + lax.broadcasted_iota(jnp.int32, shape, 0)
        query_place = at + lax.broadcasted_iota(jnp.int32, shape, 1)
        allowed = (key_place >= starts_ref[0:1, at : at + BLOCK]) & (key_place <= query_place)
        bias_ref[index, 0 : high - low, :] = jnp.where(allowed, 0.0, -1e30)


def forward_kernel(starts_ref, q_ref, k_ref, v_ref, out_ref, log_ref, bias_ref, vt_ref):
    rows = q_ref.shape[0]
    head = pl.program_id(0)

    @pl.when(head == 0)
    def _():
        fill_bias(starts_ref, bias_ref, rows)

    @pl.when(lax.rem(head, GROUP) == 0)
    def _():
        vt_ref[...] = v_ref[...].astype(jnp.float32).T.astype(jnp.bfloat16)

    for index, (at, low, high) in enumerate(windows(rows)):
        scores = dot(k_ref[low:high, :], q_ref[at : at + BLOCK, :], NT)
        scores = scores * (FACTOR * LOG2E) + bias_ref[index, 0 : high - low, :]
        top = jnp.max(scores, axis=0, keepdims=True)
        probs = jnp.exp2(scores - top)
        total = jnp.sum(probs, axis=0, keepdims=True)
        out = dot(vt_ref[:, low:high], probs.astype(jnp.bfloat16), NN)
        out_ref[at : at + BLOCK, :] = (out / total).T.astype(jnp.bfloat16)
        log_ref[0, 0:1, at : at + BLOCK] = top + jnp.log2(total)


def backward_kernel(
    starts_ref,
    q_ref,
    k_ref,
    v_ref,
    o_ref,
    g_ref,
    log_ref,
    dq_ref,
    dk_ref,
    dv_ref,
    bias_ref,
    kt_ref,
    dk_acc,
    dv_acc,
):
    rows = q_ref.shape[0]
    head = pl.program_id(0)

    @pl.when(head == 0)
    def _():
        fill_bias(starts_ref, bias_ref, rows)

    @pl.when(lax.rem(head, GROUP) == 0)
    def _():
        kt_ref[...] = k_ref[...].astype(jnp.float32).T.astype(jnp.bfloat16)
        dk_acc[...] = jnp.zeros_like(dk_acc)
        dv_acc[...] = jnp.zeros_like(dv_acc)

    for index, (at, low, high) in enumerate(windows(rows)):
        q = q_ref[at : at + BLOCK, :]
        g = g_ref[at : at + BLOCK, :]
        scores = dot(k_ref[low:high, :], q, NT)
        scores = scores * (FACTOR * LOG2E) + bias_ref[index, 0 : high - low, :]
        probs = jnp.exp2(scores - log_ref[0, 0:1, at : at + BLOCK])
        prob_grad = dot(v_ref[low:high, :], g, NT)
        product = g.astype(jnp.float32) * o_ref[at : at + BLOCK, :].astype(jnp.float32)
        delta = jnp.sum(product.T, axis=0, keepdims=True)
        score_grad = (probs * (prob_grad - delta)).astype(jnp.bfloat16)
        dv_acc[low:high, :] += dot(probs.astype(jnp.bfloat16), g, NN)
        dk_acc[low:high, :] += dot(score_grad, q, NN)
        dq = dot(kt_ref[:, low:high], score_grad, NN) * FACTOR
        dq_ref[at : at + BLOCK, :] = dq.T.astype(jnp.bfloat16)

    @pl.when(lax.rem(head, GROUP) == GROUP - 1)
    def _():
        dk_ref[...] = (dk_acc[...] * FACTOR).astype(jnp.bfloat16)
        dv_ref[...] = dv_acc[...].astype(jnp.bfloat16)


def attention_specs(rows):
    whole = pl.BlockSpec((1, rows), lambda h: (0, 0))
    one = pl.BlockSpec((rows, HEAD_SIZE), lambda h: (0, h))
    shared = pl.BlockSpec((rows, HEAD_SIZE), lambda h: (0, h // GROUP))
    logs = pl.BlockSpec((1, 1, rows), lambda h: (h, 0, 0))
    return whole, one, shared, logs


def attention_forward(starts, query, keys, values):
    rows, width = query.shape
    heads = width // HEAD_SIZE
    whole, one, shared, logs = attention_specs(rows)
    pairs = sum(high - low for _, low, high in windows(rows)) * BLOCK
    return pl.pallas_call(
        forward_kernel,
        grid=(heads,),
        in_specs=[whole, one, shared, shared],
        out_specs=[one, logs],
        out_shape=[
            jax.ShapeDtypeStruct((rows, width), jnp.bfloat16),
            jax.ShapeDtypeStruct((heads, 1, rows), jnp.float32),
        ],
        scratch_shapes=[
            pltpu.VMEM((rows // BLOCK, REACH + BLOCK, BLOCK), jnp.float32),
            pltpu.VMEM((HEAD_SIZE, rows), jnp.bfloat16),
        ],
        compiler_params=pltpu.CompilerParams(vmem_limit_bytes=40 * 1024 * 1024),
        cost_estimate=pl.CostEstimate(
            flops=heads * pairs * HEAD_SIZE * 2 * 2 * 3,
            bytes_accessed=rows * width * 2 * 3,
            transcendentals=heads * pairs,
        ),
        name="attention_forward",
    )(starts, query, keys, values)


def attention_backward(starts, query, keys, values, out, grad, logs_in):
    rows, width = query.shape
    heads = width // HEAD_SIZE
    whole, one, shared, logs = attention_specs(rows)
    pairs = sum(high - low for _, low, high in windows(rows)) * BLOCK
    return pl.pallas_call(
        backward_kernel,
        grid=(heads,),
        in_specs=[whole, one, shared, shared, one, one, logs],
        out_specs=[one, shared, shared],
        out_shape=[
            jax.ShapeDtypeStruct((rows, width), jnp.bfloat16),
            jax.ShapeDtypeStruct(keys.shape, jnp.bfloat16),
            jax.ShapeDtypeStruct(values.shape, jnp.bfloat16),
        ],
        scratch_shapes=[
            pltpu.VMEM((rows // BLOCK, REACH + BLOCK, BLOCK), jnp.float32),
            pltpu.VMEM((HEAD_SIZE, rows), jnp.bfloat16),
            pltpu.VMEM((rows, HEAD_SIZE), jnp.float32),
            pltpu.VMEM((rows, HEAD_SIZE), jnp.float32),
        ],
        compiler_params=pltpu.CompilerParams(vmem_limit_bytes=40 * 1024 * 1024),
        cost_estimate=pl.CostEstimate(
            flops=heads * pairs * HEAD_SIZE * 2 * 5 * 3,
            bytes_accessed=rows * width * 2 * 5,
            transcendentals=heads * pairs,
        ),
        name="attention_backward",
    )(starts, query, keys, values, out, grad, logs_in)


def shards(query, keys, values, out_weight, loss_grad, lengths, languages, labels):
    rows = query.shape[0]
    places = jnp.arange(rows, dtype=jnp.int32)
    order = jnp.arange(DOCS, dtype=jnp.int32)
    ends = jnp.sum(jnp.where(order[:, None] >= order[None, :], lengths[0][None, :], 0), axis=1)
    begins = ends - lengths[0]
    inside = (places[None, :] >= begins[:, None]) & (places[None, :] < ends[:, None])
    starts = jnp.sum(jnp.where(inside, begins[:, None], 0), axis=0)[None, :]
    full_grad = lax.all_gather(loss_grad, "tensor", axis=1, tiled=True)
    full_weight = lax.all_gather(out_weight, "dp", axis=1, tiled=True)
    token_lang = jnp.sum(jnp.where(inside, languages[0][:, None], 0), axis=0)
    counted = labels != -100
    lang_match = token_lang[:, None] == jnp.arange(LANGS, dtype=jnp.int32)[None, :]
    local_counts = jnp.sum((lang_match & counted[:, None]).astype(jnp.int32), axis=0)
    counts = lax.psum(local_counts, "dp").astype(jnp.float32)
    lang_weight = jnp.sqrt(jnp.sum(counts) / (LANGS * jnp.maximum(counts, 1.0)))
    token_weight = jnp.where(
        counted, jnp.sum(jnp.where(lang_match, lang_weight[None, :], 0.0), axis=1), 0.0
    )
    attention_result, logs = attention_forward(starts, query, keys, values)
    full_grad, full_weight = lax.optimization_barrier((full_grad, full_weight))
    weighted = (token_weight[:, None] * full_grad.astype(jnp.float32)).astype(jnp.bfloat16)
    local_term = dot(attention_result, weighted, TN).astype(jnp.bfloat16)
    own_rows = lax.psum_scatter(local_term, "dp", scatter_dimension=0, tiled=True)
    out_grad = dot(weighted, full_weight, NT).astype(jnp.bfloat16)
    own_rows, _ = lax.optimization_barrier((own_rows, out_grad))
    projection_gradient = lax.all_gather(own_rows, "dp", axis=0, tiled=True)
    query_gradient, key_gradient, value_gradient = attention_backward(
        starts, query, keys, values, attention_result, out_grad, logs
    )
    return (attention_result, query_gradient, key_gradient, value_gradient, projection_gradient)


def solution(mesh):
    in_specs = (
        P("dp", "tensor"),
        P("dp", "tensor"),
        P("dp", "tensor"),
        P("tensor", "dp"),
        P("dp", "tensor"),
        P("dp", None),
        P("dp", None),
        P("dp"),
    )
    out_specs = (
        P("dp", "tensor"),
        P("dp", "tensor"),
        P("dp", "tensor"),
        P("dp", "tensor"),
        P("tensor", None),
    )
    return jax.shard_map(shards, mesh=mesh, in_specs=in_specs, out_specs=out_specs, check_vma=False)
```
